32 devices in a mesh: row: 8 (over z, core), col: 4 (over y, x).
Axes of the slice: x: 2, y: 2, z: 4, core: 2. Of those that a mesh axis runs over, the one named last changes fastest.
Arguments:
- eigvecs: float32 [512, 262144], P(('row', 'col')), may hold values from -6 to 6
- panels: bfloat16 [4, 262144, 128], P('col', 'row'), may hold values from -0.01171875 to 0.01171875
- tfactors: bfloat16 [4, 128, 128], P('col'), as said below
- owners: int32 [4], replicated, may hold values from 0 to 3, as said below
- offsets: int32 [4], replicated, may hold values from 0 to 65408, as said below
Outputs:
- back: float32 [512, 262144], P('col', 'row')
The draws below stay inside these ranges and needn't reach their ends.
Inputs may be any that keep to these rules, and one draw needn't show every extreme that they name: `owners`: distinct grid columns. `offsets`: multiples of 128. `tfactors`: each matrix is upper triangular with its diagonal between 1 and 8.
All inputs are finite; a program needn't handle non-finite values.
Results may differ from the reference program's by a relative error of at most 0.0003.
Values may be sent and summed in bfloat16 or wider, within the bound.
A program may use at most 192 MiB of HBM per device.

```python
import jax
import jax.numpy as jnp
from jax import lax

N = 262144
NB = 128
K = 512
PANELS = 4
N_COL = 4


def draw_tfactors(key, part):
    key_diag = jax.random.fold_in(key, 5)
    key_above = jax.random.fold_in(key, 7)
    diagonal = jax.random.uniform(key_diag, (N_COL, NB), jnp.float32, 2.0, 6.0)
    above = jax.random.normal(key_above, (N_COL, NB, NB), jnp.float32)
    upper = jnp.triu(above, 1)
    identity = jnp.eye(NB, dtype=jnp.float32)
    return (upper + diagonal[:, :, None] * identity[None, :, :]).astype(jnp.bfloat16)


def draw_owners(key, part):
    order = jax.random.permutation(jax.random.fold_in(key, 11), N_COL)
    return order[:PANELS].astype(jnp.int32)


def draw_offsets(key, part):
    top_block = N // (4 * NB) - 1
    blocks = jax.random.randint(jax.random.fold_in(key, 23), (PANELS,), 0, top_block + 1).astype(jnp.int32)
    order = jax.random.permutation(jax.random.fold_in(key, 29), PANELS).astype(jnp.int32)
    blocks = blocks.at[order[0]].set(jnp.int32(top_block))
    blocks = blocks.at[order[1]].set(jnp.int32(0))
    return (blocks * NB).astype(jnp.int32)


def block_scale(key, extent, shards, low, high):
    loudness = 1.0
    for axis_at, parts in shards:
        draws = jax.random.uniform(jax.random.fold_in(jax.random.fold_in(key, 6), axis_at), (parts,), jnp.float32, low / len(shards), high / len(shards))
        loudness = loudness * jnp.repeat(jnp.exp(draws), extent[axis_at] // parts).reshape((-1,) + (1,) * (len(extent) - 1 - axis_at))
    return loudness


def centred(stream_key, shape, width, most, split=(), held_as=jnp.bfloat16):
    gain = block_scale(stream_key, shape, split, -0.22, 0.18) if split else 1.0
    drawn = jax.random.normal(stream_key, shape, jnp.float32) * width * gain
    return jnp.minimum(jnp.maximum(drawn, -most), most).astype(held_as)


def setup_inputs(seed: int = 0) -> dict:
    key_of = jax.random.split(jax.random.key(seed), 6)
    return {
        "eigvecs": centred(key_of[0], (K, N), 1.0, 6.0, ((0, 32),), jnp.float32),
        "panels": centred(key_of[1], (N_COL, N, NB), N ** -0.5, 0.01171875, ((0, 4), (1, 8))),
        "tfactors": draw_tfactors(jax.random.fold_in(key_of[5], 71), 0),
        "owners": draw_owners(jax.random.fold_in(key_of[5], 71), 0),
        "offsets": draw_offsets(jax.random.fold_in(key_of[5], 71), 0),
    }


def reference(eigvecs, panels, tfactors, owners, offsets):
    highest = lax.Precision.HIGHEST
    row_ids = jnp.arange(N, dtype=jnp.int32)[:, None]
    col_ids = jnp.arange(NB, dtype=jnp.int32)[None, :]
    field = eigvecs
    for panel in reversed(range(PANELS)):
        owner_col = owners[panel].astype(jnp.int32)
        stored = lax.dynamic_index_in_dim(panels, owner_col, 0, keepdims=False).astype(jnp.float32)
        triangle = lax.dynamic_index_in_dim(tfactors, owner_col, 0, keepdims=False).astype(jnp.float32)
        below = row_ids - col_ids - offsets[panel].astype(jnp.int32)
        unit = jnp.where(below == 0, jnp.float32(1.0), jnp.float32(0.0))
        reflector = jnp.where(below > 0, stored, unit)
        projection = jnp.dot(field, reflector, precision=highest, preferred_element_type=jnp.float32)
        coeffs = jnp.dot(projection, triangle.T, precision=highest, preferred_element_type=jnp.float32)
        field = field - jnp.dot(coeffs, reflector.T, precision=highest, preferred_element_type=jnp.float32)
    return field
```

```python
import jax
import jax.numpy as jnp
from jax import lax
from jax.sharding import PartitionSpec as P

PANELS = 4
GROUP = 128
TOP = 32767.0


def encode(value):
    rows, columns = value.shape
    grouped = value.reshape(rows, columns // GROUP, GROUP)
    peak = jnp.max(jnp.abs(grouped), axis=2)
    peak = jnp.maximum(peak, jnp.float32(1e-30))
    code = jnp.round(grouped * (TOP / peak)[:, :, None])
    code = jnp.clip(code, -TOP, TOP).astype(jnp.int16)
    return code.reshape(rows, columns), peak * jnp.float32(1.0 / TOP)


def decode(code, step):
    rows, columns = code.shape
    grouped = code.reshape(rows, columns // GROUP, GROUP).astype(jnp.float32)
    return (grouped * step[:, :, None]).reshape(rows, columns)


def split(value):
    high = lax.reduce_precision(value, 8, 7)
    return high.astype(jnp.bfloat16), (value - high).astype(jnp.bfloat16)


def reflector_block(stored, offset, first_row):
    row_ids = first_row + lax.broadcasted_iota(jnp.int32, stored.shape, 0)
    col_ids = lax.broadcasted_iota(jnp.int32, stored.shape, 1)
    below = row_ids - col_ids - offset
    unit = jnp.where(below == 0, jnp.bfloat16(1.0), jnp.bfloat16(0.0))
    return jnp.where(below > 0, stored, unit)


def dot(a, b, contract):
    return lax.dot_general(a, b, (contract, ((), ())), preferred_element_type=jnp.float32)


def local(eigvecs, panels, tfactors, owners, offsets):
    highest = lax.Precision.HIGHEST
    both = ("row", "col")
    n_col = lax.axis_size("col")
    stored = lax.all_to_all(panels[0], "col", split_axis=0, concat_axis=0, tiled=True)
    triangles = lax.all_gather(tfactors[0], "col")
    code, step = encode(eigvecs)
    code = lax.all_to_all(code, both, split_axis=1, concat_axis=0, tiled=True)
    step = lax.all_to_all(step, both, split_axis=1, concat_axis=0, tiled=True)
    local_rows = code.shape[1]
    first_row = (lax.axis_index("row") * n_col + lax.axis_index("col")) * local_rows
    stored = stored.reshape(n_col, local_rows, stored.shape[-1])
    reflectors = [
        reflector_block(
            lax.dynamic_index_in_dim(stored, owners[panel], 0, keepdims=False),
            offsets[panel],
            first_row,
        )
        for panel in range(PANELS)
    ]
    reflector = jnp.concatenate(reflectors, axis=1)
    nb = reflector.shape[1] // PANELS
    gram = lax.psum(dot(reflector, reflector, ((0,), (0,))), both)
    field = decode(code, step)
    high, low = split(field)
    product = dot(high, reflector, ((1,), (0,))) + dot(low, reflector, ((1,), (0,)))
    projection = lax.psum(product, both)
    coeffs = [None] * PANELS
    for panel in reversed(range(PANELS)):
        at = slice(panel * nb, (panel + 1) * nb)
        inner = projection[:, at]
        for later in range(panel + 1, PANELS):
            block = gram[later * nb : (later + 1) * nb, at]
            inner = inner - jnp.dot(coeffs[later], block, precision=highest)
        triangle = lax.dynamic_index_in_dim(triangles, owners[panel], 0, keepdims=False)
        coeffs[panel] = jnp.dot(inner, triangle.astype(jnp.float32).T, precision=highest)
    high, low = split(jnp.concatenate(coeffs, axis=1))
    change = dot(high, reflector, ((1,), (1,))) + dot(low, reflector, ((1,), (1,)))
    code, step = encode(field - change)
    code = lax.all_to_all(code, "col", split_axis=0, concat_axis=1, tiled=True)
    step = lax.all_to_all(step, "col", split_axis=0, concat_axis=1, tiled=True)
    return decode(code, step)


def solution(mesh):
    in_specs = (P(("row", "col"), None), P("col", "row", None), P("col", None, None), P(), P())
    out_specs = P("col", "row")
    return jax.shard_map(local, mesh=mesh, in_specs=in_specs, out_specs=out_specs, check_vma=False)
```

```python
import functools

import jax
import jax.numpy as jnp
from jax import lax
from jax.experimental import pallas as pl
from jax.experimental.pallas import tpu as pltpu
from jax.sharding import PartitionSpec as P

PANELS = 4
GROUP = 128
CHUNK = 1024
TOP = 32767.0
FINE = 256.0
LN2 = 0.6931471805599453
VMEM_LIMIT = 56 * 1024 * 1024


def exponents(peaks):
    return jnp.ceil(jnp.log(jnp.maximum(peaks, 1e-30)) * (FINE / LN2))


def steps_of(code):
    return jnp.exp(code.astype(jnp.int32).astype(jnp.float32) * (LN2 / FINE)) * (1.0 / TOP)


def quantize(value, inverse):
    scaled = jnp.clip(jnp.round(value * inverse), -TOP, TOP)
    return scaled.astype(jnp.int32).astype(jnp.int16)


def as_float(code):
    return code.astype(jnp.int32).astype(jnp.float32)


def encode_kernel(x_ref, code_ref):
    rows, length = x_ref.shape
    lane = lax.broadcasted_iota(jnp.int32, (rows, GROUP), 1)
    peaks = jnp.zeros((rows, GROUP), jnp.float32)
    for g in range(length // GROUP):
        part = jnp.abs(x_ref[:, g * GROUP : (g + 1) * GROUP])
        peaks = jnp.where(lane == g, jnp.max(part, axis=1, keepdims=True), peaks)
    exponent = exponents(peaks)
    code_ref[:, length:] = exponent.astype(jnp.int32).astype(jnp.int16)
    inverse = jnp.exp(exponent * (-LN2 / FINE)) * TOP
    for g in range(length // GROUP):
        at = slice(g * GROUP, (g + 1) * GROUP)
        code_ref[:, at] = quantize(x_ref[:, at], inverse[:, g : g + 1])


def encode(eigvecs, parts):
    rows, columns = eigvecs.shape
    length = columns // parts
    return pl.pallas_call(
        encode_kernel,
        grid=(parts,),
        in_specs=[pl.BlockSpec((rows, length), lambda i: (0, i))],
        out_specs=pl.BlockSpec((None, rows, length + GROUP), lambda i: (i, 0, 0)),
        out_shape=jax.ShapeDtypeStruct((parts, rows, length + GROUP), jnp.int16),
        compiler_params=pltpu.CompilerParams(vmem_limit_bytes=VMEM_LIMIT),
        cost_estimate=pl.CostEstimate(
            flops=6 * rows * columns, bytes_accessed=6 * rows * columns, transcendentals=0
        ),
        name="encode",
    )(eigvecs)


def decoded_chunk(code_ref, steps, i):
    per = CHUNK // GROUP
    rolled = pltpu.roll(steps, lax.rem(GROUP - per * i, GROUP), 1)
    return [
        as_float(code_ref[:, pl.ds(pl.multiple_of(i * CHUNK + j * GROUP, GROUP), GROUP)])
        * rolled[:, j : j + 1]
        for j in range(per)
    ]


def project_kernel(code_ref, reflector_ref, out_ref, total):
    rows, length = out_ref.shape[0], reflector_ref.shape[0]
    steps = steps_of(code_ref[:, length:])
    total[...] = jnp.zeros_like(total)

    @pl.loop(0, length // CHUNK)
    def _(i):
        value = jnp.concatenate(decoded_chunk(code_ref, steps, i), axis=1)
        high = value.astype(jnp.bfloat16)
        low = (value - high.astype(jnp.float32)).astype(jnp.bfloat16)
        block = reflector_ref[pl.ds(pl.multiple_of(i * CHUNK, CHUNK), CHUNK), :]
        total[...] += jnp.dot(
            jnp.concatenate([high, low], axis=0), block, preferred_element_type=jnp.float32
        )

    out_ref[...] = total[:rows] + total[rows:]


def project(code, reflector, rows):
    count, width = code.shape
    length, reach = reflector.shape
    return pl.pallas_call(
        project_kernel,
        grid=(count // rows,),
        in_specs=[
            pl.BlockSpec((rows, width), lambda i: (i, 0)),
            pl.BlockSpec((length, reach), lambda i: (0, 0)),
        ],
        out_specs=pl.BlockSpec((rows, reach), lambda i: (i, 0)),
        out_shape=jax.ShapeDtypeStruct((count, reach), jnp.float32),
        scratch_shapes=[pltpu.VMEM((2 * rows, reach), jnp.float32)],
        compiler_params=pltpu.CompilerParams(vmem_limit_bytes=VMEM_LIMIT),
        cost_estimate=pl.CostEstimate(
            flops=4 * count * length * reach,
            bytes_accessed=2 * count * width + 2 * length * reach,
            transcendentals=0,
        ),
        name="project",
    )(code, reflector)


def update_kernel(code_ref, coeff_ref, reflector_ref, out_ref, field, peaks):
    rows, length = field.shape
    reach = reflector_ref.shape[1]
    per = CHUNK // GROUP
    steps = steps_of(code_ref[:, length:])
    lane = lax.broadcasted_iota(jnp.int32, (rows, GROUP), 1)
    coeffs = jnp.concatenate([coeff_ref[:, :reach], coeff_ref[:, reach:]], axis=0)
    peaks[...] = jnp.zeros_like(peaks)

    @pl.loop(0, length // CHUNK)
    def _(i):
        block = reflector_ref[pl.ds(pl.multiple_of(i * CHUNK, CHUNK), CHUNK), :]
        change = lax.dot_general(
            coeffs, block, (((1,), (1,)), ((), ())), preferred_element_type=jnp.float32
        )
        change = change[:rows] + change[rows:]
        top = peaks[...]
        for j, part in enumerate(decoded_chunk(code_ref, steps, i)):
            new = part - change[:, j * GROUP : (j + 1) * GROUP]
            field[:, pl.ds(pl.multiple_of(i * CHUNK + j * GROUP, GROUP), GROUP)] = new
            top = jnp.where(lane == i * per + j, jnp.max(jnp.abs(new), axis=1, keepdims=True), top)
        peaks[...] = top

    exponent = exponents(peaks[...])
    out_ref[:, length:] = exponent.astype(jnp.int32).astype(jnp.int16)
    inverse = jnp.exp(exponent * (-LN2 / FINE)) * TOP

    @pl.loop(0, length // CHUNK)
    def _(i):
        rolled = pltpu.roll(inverse, lax.rem(GROUP - per * i, GROUP), 1)
        for j in range(per):
            at = pl.ds(pl.multiple_of(i * CHUNK + j * GROUP, GROUP), GROUP)
            out_ref[:, at] = quantize(field[:, at], rolled[:, j : j + 1])


def update(code, coeffs, reflector, rows):
    count, width = code.shape
    length, reach = reflector.shape
    return pl.pallas_call(
        update_kernel,
        grid=(count // rows,),
        in_specs=[
            pl.BlockSpec((rows, width), lambda i: (i, 0)),
            pl.BlockSpec((rows, 2 * reach), lambda i: (i, 0)),
            pl.BlockSpec((length, reach), lambda i: (0, 0)),
        ],
        out_specs=pl.BlockSpec((rows, width), lambda i: (i, 0)),
        out_shape=jax.ShapeDtypeStruct((count, width), jnp.int16),
        scratch_shapes=[
            pltpu.VMEM((rows, length), jnp.float32),
            pltpu.VMEM((rows, GROUP), jnp.float32),
        ],
        compiler_params=pltpu.CompilerParams(vmem_limit_bytes=VMEM_LIMIT),
        cost_estimate=pl.CostEstimate(
            flops=4 * count * length * reach,
            bytes_accessed=4 * count * width + 2 * length * reach,
            transcendentals=0,
        ),
        name="update",
    )(code, coeffs, reflector)


def decode_kernel(code_ref, out_ref):
    length = out_ref.shape[1]
    steps = steps_of(code_ref[:, length:])

    @pl.loop(0, length // CHUNK)
    def _(i):
        for j, part in enumerate(decoded_chunk(code_ref, steps, i)):
            out_ref[:, pl.ds(pl.multiple_of(i * CHUNK + j * GROUP, GROUP), GROUP)] = part


def decode(code, parts):
    count, width = code.shape
    rows, length = count // parts, width - GROUP
    return pl.pallas_call(
        decode_kernel,
        grid=(parts,),
        in_specs=[pl.BlockSpec((rows, width), lambda i: (i, 0))],
        out_specs=pl.BlockSpec((rows, length), lambda i: (0, i)),
        out_shape=jax.ShapeDtypeStruct((rows, parts * length), jnp.float32),
        compiler_params=pltpu.CompilerParams(vmem_limit_bytes=VMEM_LIMIT),
        cost_estimate=pl.CostEstimate(
            flops=2 * count * length, bytes_accessed=6 * count * length, transcendentals=0
        ),
        name="decode",
    )(code)


def reflector_block(stored, offset, first_row):
    row_ids = first_row + lax.broadcasted_iota(jnp.int32, stored.shape, 0)
    col_ids = lax.broadcasted_iota(jnp.int32, stored.shape, 1)
    below = row_ids - col_ids - offset
    unit = jnp.where(below == 0, jnp.bfloat16(1.0), jnp.bfloat16(0.0))
    return jnp.where(below > 0, stored, unit)


def spread_panels(stored, n_col):
    length = stored.shape[0] // n_col
    me = lax.axis_index("col")
    pieces = []
    for k in range(n_col):
        to = lax.rem(me + k, n_col)
        piece = lax.dynamic_slice_in_dim(stored, to * length, length, axis=0)
        if k:
            piece = lax.ppermute(piece, "col", [(i, (i + k) % n_col) for i in range(n_col)])
        pieces.append(piece)
    return jnp.stack(pieces)


def local(eigvecs, panels, tfactors, owners, offsets):
    highest = lax.Precision.HIGHEST
    both = ("row", "col")
    n_row, n_col = lax.axis_size("row"), lax.axis_size("col")
    n_all = n_row * n_col
    me = lax.axis_index("col")
    stored = spread_panels(panels[0], n_col)
    triangles = lax.all_gather(tfactors[0], "col")
    code = encode(eigvecs, n_all)
    code = lax.all_to_all(code, both, split_axis=0, concat_axis=0, tiled=True)
    code = code.reshape(-1, code.shape[-1])
    count, rows = code.shape[0], code.shape[0] // n_col
    length = stored.shape[1]
    first_row = (lax.axis_index("row") * n_col + me) * length
    reflectors = [
        reflector_block(
            lax.dynamic_index_in_dim(
                stored, lax.rem(me - owners[panel] + n_col, n_col), 0, keepdims=False
            ),
            offsets[panel],
            first_row,
        )
        for panel in range(PANELS)
    ]
    reflector = jnp.concatenate(reflectors, axis=1)
    nb = reflector.shape[1] // PANELS
    gram = lax.psum(
        lax.dot_general(
            reflector, reflector, (((0,), (0,)), ((), ())), preferred_element_type=jnp.float32
        ),
        both,
    )
    identity = jnp.eye(PANELS * nb, dtype=jnp.float32)
    columns = [None] * PANELS
    for panel in reversed(range(PANELS)):
        at = slice(panel * nb, (panel + 1) * nb)
        inner = identity[:, at]
        for later in range(panel + 1, PANELS):
            block = gram[later * nb : (later + 1) * nb, at]
            inner = inner - jnp.dot(columns[later], block, precision=highest)
        triangle = lax.dynamic_index_in_dim(triangles, owners[panel], 0, keepdims=False)
        columns[panel] = jnp.dot(inner, triangle.astype(jnp.float32).T, precision=highest)
    mixing = jnp.concatenate(columns, axis=1)

    partial_sums = project(code, reflector, rows)
    partial_sums = lax.all_to_all(partial_sums, both, split_axis=0, concat_axis=0, tiled=True)
    projection = jnp.sum(partial_sums.reshape(n_all, count // n_all, -1), axis=0)
    coeffs = jnp.dot(projection, mixing, precision=highest)
    high = lax.reduce_precision(coeffs, 8, 7)
    pair = jnp.concatenate([high, coeffs - high], axis=1).astype(jnp.bfloat16)
    pair = lax.all_gather(pair, both, tiled=True)
    code = update(code, pair, reflector, rows)
    code = lax.all_to_all(code, "col", split_axis=0, concat_axis=0, tiled=True)
    return decode(code, n_col)


def solution(mesh):
    in_specs = (P(("row", "col"), None), P("col", "row", None), P("col", None, None), P(), P())
    out_specs = P("col", "row")
    return jax.shard_map(local, mesh=mesh, in_specs=in_specs, out_specs=out_specs, check_vma=False)
```

```python
import functools

import jax
import jax.numpy as jnp
from jax import lax
from jax.experimental import pallas as pl
from jax.experimental.pallas import tpu as pltpu
from jax.sharding import PartitionSpec as P

PANELS = 4
GROUP = 128
CHUNK = 1024
TOP = 32767.0
FINE = 256.0
LN2 = 0.6931471805599453
VMEM_LIMIT = 56 * 1024 * 1024


def exponents(peaks):
    return jnp.ceil(jnp.log(jnp.maximum(peaks, 1e-30)) * (FINE / LN2))


def steps_of(code):
    return jnp.exp(code.astype(jnp.int32).astype(jnp.float32) * (LN2 / FINE)) * (1.0 / TOP)


def quantize(value, inverse):
    scaled = jnp.clip(jnp.round(value * inverse), -TOP, TOP)
    return scaled.astype(jnp.int32).astype(jnp.int16)


def as_float(code):
    return code.astype(jnp.int32).astype(jnp.float32)


def encode_kernel(x_ref, code_ref):
    rows, length = x_ref.shape
    peaks = jnp.zeros((rows, GROUP), jnp.float32)
    for g in range(length // GROUP):
        peaks = jnp.maximum(peaks, jnp.abs(x_ref[:, g * GROUP : (g + 1) * GROUP]))
    exponent = exponents(peaks)
    code_ref[:, length:] = exponent.astype(jnp.int32).astype(jnp.int16)
    inverse = jnp.exp(exponent * (-LN2 / FINE)) * TOP
    for g in range(length // GROUP):
        at = slice(g * GROUP, (g + 1) * GROUP)
        code_ref[:, at] = quantize(x_ref[:, at], inverse)


def encode(eigvecs, parts, half, halves):
    rows, columns = eigvecs.shape
    rows, length = rows // halves, columns // parts
    return pl.pallas_call(
        encode_kernel,
        grid=(parts,),
        in_specs=[pl.BlockSpec((rows, length), lambda i: (half, i))],
        out_specs=pl.BlockSpec((None, rows, length + GROUP), lambda i: (i, 0, 0)),
        out_shape=jax.ShapeDtypeStruct((parts, rows, length + GROUP), jnp.int16),
        compiler_params=pltpu.CompilerParams(vmem_limit_bytes=VMEM_LIMIT),
        cost_estimate=pl.CostEstimate(
            flops=6 * rows * columns, bytes_accessed=6 * rows * columns, transcendentals=0
        ),
        name="encode",
    )(eigvecs)


def lanes(start):
    return pl.ds(pl.multiple_of(start, GROUP), GROUP)


def decoded_chunk(code_ref, steps, i):
    return [
        as_float(code_ref[:, lanes(i * CHUNK + j * GROUP)]) * steps
        for j in range(CHUNK // GROUP)
    ]


def project_kernel(code_ref, reflector_ref, out_ref, total):
    rows, length = out_ref.shape[0], reflector_ref.shape[0]
    steps = steps_of(code_ref[:, length:])
    total[...] = jnp.zeros_like(total)

    @pl.loop(0, length // CHUNK)
    def _(i):
        value = jnp.concatenate(decoded_chunk(code_ref, steps, i), axis=1)
        high = value.astype(jnp.bfloat16)
        low = (value - high.astype(jnp.float32)).astype(jnp.bfloat16)
        block = reflector_ref[pl.ds(pl.multiple_of(i * CHUNK, CHUNK), CHUNK), :]
        total[...] += jnp.dot(
            jnp.concatenate([high, low], axis=0), block, preferred_element_type=jnp.float32
        )

    out_ref[...] = total[:rows] + total[rows:]


def project(code, reflector, rows):
    count, width = code.shape
    length, reach = reflector.shape
    return pl.pallas_call(
        project_kernel,
        grid=(count // rows,),
        in_specs=[
            pl.BlockSpec((rows, width), lambda i: (i, 0)),
            pl.BlockSpec((length, reach), lambda i: (0, 0)),
        ],
        out_specs=pl.BlockSpec((rows, reach), lambda i: (i, 0)),
        out_shape=jax.ShapeDtypeStruct((count, reach), jnp.float32),
        scratch_shapes=[pltpu.VMEM((2 * rows, reach), jnp.float32)],
        compiler_params=pltpu.CompilerParams(vmem_limit_bytes=VMEM_LIMIT),
        cost_estimate=pl.CostEstimate(
            flops=4 * count * length * reach,
            bytes_accessed=2 * count * width + 2 * length * reach,
            transcendentals=0,
        ),
        name="project",
    )(code, reflector)


def update_kernel(code_ref, coeff_ref, reflector_ref, out_ref, field, peaks):
    rows, length = field.shape
    reach = reflector_ref.shape[1]
    steps = steps_of(code_ref[:, length:])
    coeffs = jnp.concatenate([coeff_ref[:, :reach], coeff_ref[:, reach:]], axis=0)
    peaks[...] = jnp.zeros_like(peaks)

    @pl.loop(0, length // CHUNK)
    def _(i):
        block = reflector_ref[pl.ds(pl.multiple_of(i * CHUNK, CHUNK), CHUNK), :]
        change = lax.dot_general(
            coeffs, block, (((1,), (1,)), ((), ())), preferred_element_type=jnp.float32
        )
        change = change[:rows] + change[rows:]
        top = peaks[...]
        for j, part in enumerate(decoded_chunk(code_ref, steps, i)):
            new = part - change[:, j * GROUP : (j + 1) * GROUP]
            field[:, lanes(i * CHUNK + j * GROUP)] = new
            top = jnp.maximum(top, jnp.abs(new))
        peaks[...] = top

    exponent = exponents(peaks[...])
    out_ref[:, length:] = exponent.astype(jnp.int32).astype(jnp.int16)
    inverse = jnp.exp(exponent * (-LN2 / FINE)) * TOP

    @pl.loop(0, length // CHUNK)
    def _(i):
        for j in range(CHUNK // GROUP):
            at = lanes(i * CHUNK + j * GROUP)
            out_ref[:, at] = quantize(field[:, at], inverse)


def update(code, coeffs, reflector, rows):
    count, width = code.shape
    length, reach = reflector.shape
    return pl.pallas_call(
        update_kernel,
        grid=(count // rows,),
        in_specs=[
            pl.BlockSpec((rows, width), lambda i: (i, 0)),
            pl.BlockSpec((rows, 2 * reach), lambda i: (i, 0)),
            pl.BlockSpec((length, reach), lambda i: (0, 0)),
        ],
        out_specs=pl.BlockSpec((rows, width), lambda i: (i, 0)),
        out_shape=jax.ShapeDtypeStruct((count, width), jnp.int16),
        scratch_shapes=[
            pltpu.VMEM((rows, length), jnp.float32),
            pltpu.VMEM((rows, GROUP), jnp.float32),
        ],
        compiler_params=pltpu.CompilerParams(vmem_limit_bytes=VMEM_LIMIT),
        cost_estimate=pl.CostEstimate(
            flops=4 * count * length * reach,
            bytes_accessed=4 * count * width + 2 * length * reach,
            transcendentals=0,
        ),
        name="update",
    )(code, coeffs, reflector)


def decode_kernel(run, *refs):
    out_ref, code_refs = refs[-1], refs[:-1]
    length, halves = out_ref.shape[1], len(code_refs)
    for half, code_ref in enumerate(code_refs):
        steps = steps_of(code_ref[:, length:])

        @pl.loop(0, length // CHUNK)
        def _(i):
            for j, part in enumerate(decoded_chunk(code_ref, steps, i)):
                at = lanes(i * CHUNK + j * GROUP)
                for k in range(part.shape[0] // run):
                    to = (k * halves + half) * run
                    out_ref[to : to + run, at] = part[k * run : (k + 1) * run]


def decode(codes, parts, run):
    count, width = codes[0].shape
    rows, length = count // parts, width - GROUP
    total = rows * len(codes)
    return pl.pallas_call(
        functools.partial(decode_kernel, rows if len(codes) == 1 else run),
        grid=(parts,),
        in_specs=[pl.BlockSpec((rows, width), lambda i: (i, 0)) for _ in codes],
        out_specs=pl.BlockSpec((total, length), lambda i: (0, i)),
        out_shape=jax.ShapeDtypeStruct((total, parts * length), jnp.float32),
        compiler_params=pltpu.CompilerParams(vmem_limit_bytes=VMEM_LIMIT),
        cost_estimate=pl.CostEstimate(
            flops=2 * total * parts * length,
            bytes_accessed=6 * total * parts * length,
            transcendentals=0,
        ),
        name="decode",
    )(*codes)


def reflector_block(stored, offset, first_row):
    row_ids = first_row + lax.broadcasted_iota(jnp.int32, stored.shape, 0)
    col_ids = lax.broadcasted_iota(jnp.int32, stored.shape, 1)
    below = row_ids - col_ids - offset
    unit = jnp.where(below == 0, jnp.bfloat16(1.0), jnp.bfloat16(0.0))
    return jnp.where(below > 0, stored, unit)


def spread_panels(stored, n_col):
    length = stored.shape[0] // n_col
    me = lax.axis_index("col")
    pieces = []
    for k in range(n_col):
        to = lax.rem(me + k, n_col)
        piece = lax.dynamic_slice_in_dim(stored, to * length, length, axis=0)
        if k:
            piece = lax.ppermute(piece, "col", [(i, (i + k) % n_col) for i in range(n_col)])
        pieces.append(piece)
    return jnp.stack(pieces)


def local(eigvecs, panels, tfactors, owners, offsets):
    highest = lax.Precision.HIGHEST
    both = ("row", "col")
    n_row, n_col = lax.axis_size("row"), lax.axis_size("col")
    n_all = n_row * n_col
    me = lax.axis_index("col")
    stored = spread_panels(panels[0], n_col)
    triangles = lax.all_gather(tfactors[0], "col")
    mine = eigvecs.shape[0]
    halves = 2 if mine % 16 == 0 else 1
    run = mine // halves
    codes = []
    for half in range(halves):
        code = encode(eigvecs, n_all, half, halves)
        code = lax.all_to_all(code, both, split_axis=0, concat_axis=0, tiled=True)
        codes.append(code.reshape(n_all * run, code.shape[-1]))
    rows = n_row * run
    length = stored.shape[1]
    first_row = (lax.axis_index("row") * n_col + me) * length
    reflectors = [
        reflector_block(
            lax.dynamic_index_in_dim(
                stored, lax.rem(me - owners[panel] + n_col, n_col), 0, keepdims=False
            ),
            offsets[panel],
            first_row,
        )
        for panel in range(PANELS)
    ]
    reflector = jnp.concatenate(reflectors, axis=1)
    nb = reflector.shape[1] // PANELS
    sums = lax.dot_general(
        reflector, reflector, (((0,), (0,)), ((), ())), preferred_element_type=jnp.float32
    )
    pairs = [(q, p) for p in range(PANELS) for q in range(p + 1, PANELS)]
    sums = [sums[q * nb : (q + 1) * nb, p * nb : (p + 1) * nb] for q, p in pairs]
    sums = lax.psum(jnp.concatenate(sums, axis=0), both)
    gram = {pair: sums[i * nb : (i + 1) * nb] for i, pair in enumerate(pairs)}
    identity = jnp.eye(PANELS * nb, dtype=jnp.float32)
    columns = [None] * PANELS
    for panel in reversed(range(PANELS)):
        at = slice(panel * nb, (panel + 1) * nb)
        inner = identity[:, at]
        for later in range(panel + 1, PANELS):
            inner = inner - jnp.dot(columns[later], gram[later, panel], precision=highest)
        triangle = lax.dynamic_index_in_dim(triangles, owners[panel], 0, keepdims=False)
        columns[panel] = jnp.dot(inner, triangle.astype(jnp.float32).T, precision=highest)
    mixing = jnp.concatenate(columns, axis=1)

    for half in range(halves):
        part = project(codes[half], reflector, rows)
        if half < halves - 1:
            projection = lax.psum_scatter(part, both, scatter_dimension=0, tiled=True)
        else:
            part = lax.all_to_all(part, both, split_axis=0, concat_axis=0, tiled=True)
            projection = jnp.sum(part.reshape(n_all, run, -1), axis=0)
        coeffs = jnp.dot(projection, mixing, precision=highest)
        high = lax.reduce_precision(coeffs, 8, 7)
        pair = jnp.concatenate([high, coeffs - high], axis=1).astype(jnp.bfloat16)
        pair = lax.all_gather(pair, both, tiled=True)
        code = update(codes[half], pair, reflector, rows)
        codes[half] = lax.all_to_all(code, "col", split_axis=0, concat_axis=0, tiled=True)
    return decode(codes, n_col, run)


def solution(mesh):
    in_specs = (P(("row", "col"), None), P("col", "row", None), P("col", None, None), P(), P())
    out_specs = P("col", "row")
    return jax.shard_map(local, mesh=mesh, in_specs=in_specs, out_specs=out_specs, check_vma=False)
```

```python
import jax
import jax.numpy as jnp
from jax import lax
from jax.experimental import pallas as pl
from jax.experimental.pallas import tpu as pltpu
from jax.sharding import PartitionSpec as P

PANELS = 4
GROUP = 128
CHUNK = 1024
TOP = 32760.0
FINE = 256.0
LN2 = 0.6931471805599453
PAIRS = [(q, p) for p in range(PANELS) for q in range(p + 1, PANELS)]
VMEM_LIMIT = 56 * 1024 * 1024


def exponents(peaks):
    return jnp.ceil(jnp.log(jnp.maximum(peaks, 1e-30)) * (FINE / LN2))


def steps_of(code):
    return jnp.exp(code.astype(jnp.int32).astype(jnp.float32) * (LN2 / FINE)) * (1.0 / TOP)


def quantize(value, inverse):
    return ((value * inverse + 32768.5).astype(jnp.int32) - 32768).astype(jnp.int16)


def as_float(code):
    return code.astype(jnp.int32).astype(jnp.float32)


def encode_kernel(x_ref, code_ref):
    parts, rows, width = code_ref.shape
    length = width - GROUP

    @pl.loop(0, parts)
    def _(part):
        peaks = jnp.zeros((rows, GROUP), jnp.float32)
        for g in range(length // GROUP):
            peaks = jnp.maximum(peaks, jnp.abs(x_ref[:, lanes(part * length + g * GROUP)]))
        exponent = exponents(peaks)
        code_ref[part, :, length:] = exponent.astype(jnp.int32).astype(jnp.int16)
        inverse = jnp.exp(exponent * (-LN2 / FINE)) * TOP
        for g in range(length // GROUP):
            value = x_ref[:, lanes(part * length + g * GROUP)]
            code_ref[part, :, g * GROUP : (g + 1) * GROUP] = quantize(value, inverse)


def encode(eigvecs, parts):
    rows, columns = eigvecs.shape
    length = columns // parts
    at_once = 4 if parts % 4 == 0 else 1
    return pl.pallas_call(
        encode_kernel,
        grid=(parts // at_once,),
        in_specs=[pl.BlockSpec((rows, at_once * length), lambda i: (0, i))],
        out_specs=pl.BlockSpec((at_once, rows, length + GROUP), lambda i: (i, 0, 0)),
        out_shape=jax.ShapeDtypeStruct((parts, rows, length + GROUP), jnp.int16),
        compiler_params=pltpu.CompilerParams(vmem_limit_bytes=VMEM_LIMIT),
        cost_estimate=pl.CostEstimate(
            flops=6 * rows * columns, bytes_accessed=6 * rows * columns, transcendentals=0
        ),
        name="encode",
    )(eigvecs)


def lanes(start):
    return pl.ds(pl.multiple_of(start, GROUP), GROUP)


def decoded_chunk(code_ref, steps, i):
    return [
        as_float(code_ref[:, lanes(i * CHUNK + j * GROUP)]) * steps
        for j in range(CHUNK // GROUP)
    ]


def project_kernel(code_ref, reflector_ref, out_ref, total):
    rows, length = out_ref.shape[0], reflector_ref.shape[0]
    steps = steps_of(code_ref[:, length:])
    total[...] = jnp.zeros_like(total)

    @pl.loop(0, length // CHUNK)
    def _(i):
        value = jnp.concatenate(decoded_chunk(code_ref, steps, i), axis=1)
        high = value.astype(jnp.bfloat16)
        low = (value - high.astype(jnp.float32)).astype(jnp.bfloat16)
        block = reflector_ref[pl.ds(pl.multiple_of(i * CHUNK, CHUNK), CHUNK), :]
        total[...] += jnp.dot(
            jnp.concatenate([high, low], axis=0), block, preferred_element_type=jnp.float32
        )

    out_ref[...] = total[:rows] + total[rows:]


def project(code, reflector, rows):
    count, width = code.shape
    length, reach = reflector.shape
    return pl.pallas_call(
        project_kernel,
        grid=(count // rows,),
        in_specs=[
            pl.BlockSpec((rows, width), lambda i: (i, 0)),
            pl.BlockSpec((length, reach), lambda i: (0, 0)),
        ],
        out_specs=pl.BlockSpec((rows, reach), lambda i: (i, 0)),
        out_shape=jax.ShapeDtypeStruct((count, reach), jnp.float32),
        scratch_shapes=[pltpu.VMEM((2 * rows, reach), jnp.float32)],
        compiler_params=pltpu.CompilerParams(vmem_limit_bytes=VMEM_LIMIT),
        cost_estimate=pl.CostEstimate(
            flops=4 * count * length * reach,
            bytes_accessed=2 * count * width + 2 * length * reach,
            transcendentals=0,
        ),
        name="project",
    )(code, reflector)


def update_kernel(code_ref, coeff_ref, reflector_ref, out_ref, field, peaks):
    rows, length = field.shape
    reach = reflector_ref.shape[1]
    steps = steps_of(code_ref[:, length:])
    coeffs = jnp.concatenate([coeff_ref[:, :reach], coeff_ref[:, reach:]], axis=0)
    peaks[...] = jnp.zeros_like(peaks)

    @pl.loop(0, length // CHUNK)
    def _(i):
        block = reflector_ref[pl.ds(pl.multiple_of(i * CHUNK, CHUNK), CHUNK), :]
        change = lax.dot_general(
            coeffs, block, (((1,), (1,)), ((), ())), preferred_element_type=jnp.float32
        )
        change = change[:rows] + change[rows:]
        top = peaks[...]
        for j, part in enumerate(decoded_chunk(code_ref, steps, i)):
            new = part - change[:, j * GROUP : (j + 1) * GROUP]
            field[:, lanes(i * CHUNK + j * GROUP)] = new
            top = jnp.maximum(top, jnp.abs(new))
        peaks[...] = top

    exponent = exponents(peaks[...])
    out_ref[:, length:] = exponent.astype(jnp.int32).astype(jnp.int16)
    inverse = jnp.exp(exponent * (-LN2 / FINE)) * TOP

    @pl.loop(0, length // CHUNK)
    def _(i):
        for j in range(CHUNK // GROUP):
            at = lanes(i * CHUNK + j * GROUP)
            out_ref[:, at] = quantize(field[:, at], inverse)


def update(code, coeffs, reflector, rows):
    count, width = code.shape
    length, reach = reflector.shape
    return pl.pallas_call(
        update_kernel,
        grid=(count // rows,),
        in_specs=[
            pl.BlockSpec((rows, width), lambda i: (i, 0)),
            pl.BlockSpec((rows, 2 * reach), lambda i: (i, 0)),
            pl.BlockSpec((length, reach), lambda i: (0, 0)),
        ],
        out_specs=pl.BlockSpec((rows, width), lambda i: (i, 0)),
        out_shape=jax.ShapeDtypeStruct((count, width), jnp.int16),
        scratch_shapes=[
            pltpu.VMEM((rows, length), jnp.float32),
            pltpu.VMEM((rows, GROUP), jnp.float32),
        ],
        compiler_params=pltpu.CompilerParams(vmem_limit_bytes=VMEM_LIMIT),
        cost_estimate=pl.CostEstimate(
            flops=4 * count * length * reach,
            bytes_accessed=4 * count * width + 2 * length * reach,
            transcendentals=0,
        ),
        name="update",
    )(code, coeffs, reflector)


def decode_kernel(code_ref, out_ref):
    length = out_ref.shape[1]
    steps = steps_of(code_ref[:, length:])

    @pl.loop(0, length // CHUNK)
    def _(i):
        for j, part in enumerate(decoded_chunk(code_ref, steps, i)):
            out_ref[:, lanes(i * CHUNK + j * GROUP)] = part


def decode(code, parts):
    count, width = code.shape
    rows, length = count // parts, width - GROUP
    return pl.pallas_call(
        decode_kernel,
        grid=(parts,),
        in_specs=[pl.BlockSpec((rows, width), lambda i: (i, 0))],
        out_specs=pl.BlockSpec((rows, length), lambda i: (0, i)),
        out_shape=jax.ShapeDtypeStruct((rows, parts * length), jnp.float32),
        compiler_params=pltpu.CompilerParams(vmem_limit_bytes=VMEM_LIMIT),
        cost_estimate=pl.CostEstimate(
            flops=2 * count * length, bytes_accessed=6 * count * length, transcendentals=0
        ),
        name="decode",
    )(code)


def reflect_kernel(source_ref, shift_ref, *refs):
    pieces, reflector_ref, gram_ref = refs[:-2], refs[-2], refs[-1]
    rows, nb = pieces[0].shape
    first = pl.program_id(0) * rows
    gap = lax.broadcasted_iota(jnp.int32, (rows, nb), 0) - lax.broadcasted_iota(
        jnp.int32, (rows, nb), 1
    )
    for panel in range(PANELS):
        stored = pieces[0][...].astype(jnp.float32)
        for k in range(1, len(pieces)):
            other = pieces[k][...].astype(jnp.float32)
            stored = jnp.where(source_ref[panel] == k, other, stored)
        below = gap + (first - shift_ref[panel])
        unit = jnp.where(below == 0, 1.0, 0.0)
        block = jnp.where(below > 0, stored, unit).astype(jnp.bfloat16)
        reflector_ref[:, panel * nb : (panel + 1) * nb] = block
    block = reflector_ref[...]
    product = lax.dot_general(
        block, block, (((0,), (0,)), ((), ())), preferred_element_type=jnp.float32
    )

    @pl.when(pl.program_id(0) == 0)
    def _():
        gram_ref[...] = product

    @pl.when(pl.program_id(0) > 0)
    def _():
        gram_ref[...] += product


def reflect(pieces, source, shift):
    length, nb = pieces[0].shape
    rows, reach = min(CHUNK, length), PANELS * nb
    scalars = pl.BlockSpec(memory_space=pltpu.SMEM)
    return pl.pallas_call(
        reflect_kernel,
        grid=(length // rows,),
        in_specs=[scalars, scalars] + [pl.BlockSpec((rows, nb), lambda i: (i, 0)) for _ in pieces],
        out_specs=[
            pl.BlockSpec((rows, reach), lambda i: (i, 0)),
            pl.BlockSpec((reach, reach), lambda i: (0, 0)),
        ],
        out_shape=[
            jax.ShapeDtypeStruct((length, reach), jnp.bfloat16),
            jax.ShapeDtypeStruct((reach, reach), jnp.float32),
        ],
        compiler_params=pltpu.CompilerParams(vmem_limit_bytes=VMEM_LIMIT),
        cost_estimate=pl.CostEstimate(
            flops=2 * length * reach * reach, bytes_accessed=4 * length * reach, transcendentals=0
        ),
        name="reflect",
    )(source, shift, *pieces)


def solve_kernel(projection_ref, gram_ref, triangle_ref, out_ref):
    highest = lax.Precision.HIGHEST
    nb = triangle_ref.shape[1]
    reach = PANELS * nb
    coeffs = [None] * PANELS
    for panel in reversed(range(PANELS)):
        inner = projection_ref[:, panel * nb : (panel + 1) * nb]
        for later in range(panel + 1, PANELS):
            i, j = divmod(PAIRS.index((later, panel)), PANELS)
            block = gram_ref[i * nb : (i + 1) * nb, j * nb : (j + 1) * nb]
            inner = inner - jnp.dot(
                coeffs[later], block, precision=highest, preferred_element_type=jnp.float32
            )
        coeffs[panel] = lax.dot_general(
            inner,
            triangle_ref[panel].astype(jnp.float32),
            (((1,), (1,)), ((), ())),
            precision=highest,
            preferred_element_type=jnp.float32,
        )
        at = panel * nb
        high = coeffs[panel].astype(jnp.bfloat16)
        low = (coeffs[panel] - high.astype(jnp.float32)).astype(jnp.bfloat16)
        out_ref[:, at : at + nb] = high
        out_ref[:, reach + at : reach + at + nb] = low


def solve(projection, gram, triangles):
    count, reach = projection.shape
    return pl.pallas_call(
        solve_kernel,
        in_specs=[pl.BlockSpec(memory_space=pltpu.VMEM)] * 3,
        out_specs=pl.BlockSpec(memory_space=pltpu.VMEM),
        out_shape=jax.ShapeDtypeStruct((count, 2 * reach), jnp.bfloat16),
        compiler_params=pltpu.CompilerParams(vmem_limit_bytes=VMEM_LIMIT),
        name="solve",
    )(projection, gram, triangles)


def spread_panels(stored, n_col):
    length = stored.shape[0] // n_col
    me = lax.axis_index("col")
    pieces = []
    for k in range(n_col):
        to = lax.rem(me + k, n_col)
        piece = lax.dynamic_slice_in_dim(stored, to * length, length, axis=0)
        if k:
            piece = lax.ppermute(piece, "col", [(i, (i + k) % n_col) for i in range(n_col)])
        pieces.append(piece)
    return pieces


def local(eigvecs, panels, tfactors, owners, offsets):
    both = ("row", "col")
    n_col = lax.axis_size("col")
    n_all = lax.axis_size("row") * n_col
    me = lax.axis_index("col")
    pieces = spread_panels(panels[0], n_col)
    triangles = lax.all_gather(tfactors[0], "col")
    triangles = jnp.take(triangles, owners, axis=0)
    code = encode(eigvecs, n_all)
    code = lax.all_to_all(code, both, split_axis=0, concat_axis=0, tiled=True)
    code = code.reshape(-1, code.shape[-1])

    length, nb = pieces[0].shape
    first_row = (lax.axis_index("row") * n_col + me) * length
    reflector, gram = reflect(pieces, lax.rem(me - owners + n_col, n_col), offsets - first_row)
    blocks = [gram[q * nb : (q + 1) * nb, p * nb : (p + 1) * nb] for q, p in PAIRS]
    blocks += [jnp.zeros_like(blocks[0])] * (-len(blocks) % PANELS)
    packed = [
        jnp.concatenate(blocks[i : i + PANELS], axis=1) for i in range(0, len(blocks), PANELS)
    ]
    packed = jnp.concatenate(packed, axis=0)

    count = code.shape[0]
    rows = min(count, 256)
    projection = project(code, reflector, rows)
    own = count // n_all
    sums = jnp.concatenate(
        [projection.reshape(n_all, own, -1), packed.reshape(n_all, -1, packed.shape[1])], axis=1
    )
    sums = lax.all_to_all(sums, both, split_axis=0, concat_axis=0, tiled=True)
    sums = jnp.sum(sums, axis=0)
    sums = jnp.broadcast_to(sums[None], (n_all,) + sums.shape)
    sums = lax.all_to_all(sums, both, split_axis=0, concat_axis=0, tiled=True)
    coeffs = solve(
        sums[:, :own].reshape(projection.shape), sums[:, own:].reshape(packed.shape), triangles
    )
    code = update(code, coeffs, reflector, rows)
    code = lax.all_to_all(code, "col", split_axis=0, concat_axis=0, tiled=True)
    return decode(code, n_col)


def solution(mesh):
    in_specs = (P(("row", "col"), None), P("col", "row", None), P("col", None, None), P(), P())
    out_specs = P("col", "row")
    return jax.shard_map(local, mesh=mesh, in_specs=in_specs, out_specs=out_specs, check_vma=False)
```

```python
import jax
import jax.numpy as jnp
from jax import lax
from jax.experimental import pallas as pl
from jax.experimental.pallas import tpu as pltpu
from jax.sharding import PartitionSpec as P

PANELS = 4
GROUP = 128
CHUNK = 1024
TOP = 32760.0
FINE = 256.0
LN2 = 0.6931471805599453
PAIRS = [(q, p) for p in range(PANELS) for q in range(p + 1, PANELS)]
VMEM_LIMIT = 56 * 1024 * 1024


def exponents(peaks):
    return jnp.ceil(jnp.log(jnp.maximum(peaks, 1e-30)) * (FINE / LN2))


def steps_of(code):
    return jnp.exp(code.astype(jnp.int32).astype(jnp.float32) * (LN2 / FINE)) * (1.0 / TOP)


def quantize(value, inverse):
    return ((value * inverse + 32768.5).astype(jnp.int32) - 32768).astype(jnp.int16)


def as_float(code):
    return code.astype(jnp.int32).astype(jnp.float32)


def encode_kernel(x_ref, code_ref):
    parts, rows, width = code_ref.shape
    length = width - GROUP

    @pl.loop(0, parts)
    def _(part):
        peaks = jnp.zeros((rows, GROUP), jnp.float32)
        for g in range(length // GROUP):
            peaks = jnp.maximum(peaks, jnp.abs(x_ref[:, lanes(part * length + g * GROUP)]))
        exponent = exponents(peaks)
        code_ref[part, :, length:] = exponent.astype(jnp.int32).astype(jnp.int16)
        inverse = jnp.exp(exponent * (-LN2 / FINE)) * TOP
        for g in range(length // GROUP):
            value = x_ref[:, lanes(part * length + g * GROUP)]
            code_ref[part, :, g * GROUP : (g + 1) * GROUP] = quantize(value, inverse)


def encode(eigvecs, parts):
    rows, columns = eigvecs.shape
    length = columns // parts
    at_once = 4 if parts % 4 == 0 else 1
    return pl.pallas_call(
        encode_kernel,
        grid=(parts // at_once,),
        in_specs=[pl.BlockSpec((rows, at_once * length), lambda i: (0, i))],
        out_specs=pl.BlockSpec((at_once, rows, length + GROUP), lambda i: (i, 0, 0)),
        out_shape=jax.ShapeDtypeStruct((parts, rows, length + GROUP), jnp.int16),
        compiler_params=pltpu.CompilerParams(vmem_limit_bytes=VMEM_LIMIT),
        cost_estimate=pl.CostEstimate(
            flops=6 * rows * columns, bytes_accessed=6 * rows * columns, transcendentals=0
        ),
        name="encode",
    )(eigvecs)


def lanes(start):
    return pl.ds(pl.multiple_of(start, GROUP), GROUP)


def decoded_chunk(code_ref, steps, i):
    return [
        as_float(code_ref[:, lanes(i * CHUNK + j * GROUP)]) * steps
        for j in range(CHUNK // GROUP)
    ]


def project_kernel(code_ref, reflector_ref, out_ref, total):
    rows, length = out_ref.shape[0], reflector_ref.shape[0]
    steps = steps_of(code_ref[:, length:])
    total[...] = jnp.zeros_like(total)

    @pl.loop(0, length // CHUNK)
    def _(i):
        value = jnp.concatenate(decoded_chunk(code_ref, steps, i), axis=1)
        high = value.astype(jnp.bfloat16)
        low = (value - high.astype(jnp.float32)).astype(jnp.bfloat16)
        block = reflector_ref[pl.ds(pl.multiple_of(i * CHUNK, CHUNK), CHUNK), :]
        total[...] += jnp.dot(
            jnp.concatenate([high, low], axis=0), block, preferred_element_type=jnp.float32
        )

    out_ref[...] = total[:rows] + total[rows:]


def project(code, reflector, rows):
    count, width = code.shape
    length, reach = reflector.shape
    return pl.pallas_call(
        project_kernel,
        grid=(count // rows,),
        in_specs=[
            pl.BlockSpec((rows, width), lambda i: (i, 0)),
            pl.BlockSpec((length, reach), lambda i: (0, 0)),
        ],
        out_specs=pl.BlockSpec((rows, reach), lambda i: (i, 0)),
        out_shape=jax.ShapeDtypeStruct((count, reach), jnp.float32),
        scratch_shapes=[pltpu.VMEM((2 * rows, reach), jnp.float32)],
        compiler_params=pltpu.CompilerParams(vmem_limit_bytes=VMEM_LIMIT),
        cost_estimate=pl.CostEstimate(
            flops=4 * count * length * reach,
            bytes_accessed=2 * count * width + 2 * length * reach,
            transcendentals=0,
        ),
        name="project",
    )(code, reflector)


def update_kernel(code_ref, coeff_ref, reflector_ref, out_ref, field, peaks):
    rows, length = field.shape
    reach = reflector_ref.shape[1]

    def joined(value):
        return value.reshape(rows, value.shape[-1])

    steps = joined(steps_of(code_ref[:, :, length:]))
    coeffs = jnp.concatenate(
        [joined(coeff_ref[:, :, :reach]), joined(coeff_ref[:, :, reach:])], axis=0
    )
    peaks[...] = jnp.zeros_like(peaks)

    @pl.loop(0, length // CHUNK)
    def _(i):
        block = reflector_ref[pl.ds(pl.multiple_of(i * CHUNK, CHUNK), CHUNK), :]
        change = lax.dot_general(
            coeffs, block, (((1,), (1,)), ((), ())), preferred_element_type=jnp.float32
        )
        change = change[:rows] + change[rows:]
        top = peaks[...]
        for j in range(CHUNK // GROUP):
            at = lanes(i * CHUNK + j * GROUP)
            part = joined(as_float(code_ref[:, :, at])) * steps
            new = part - change[:, j * GROUP : (j + 1) * GROUP]
            field[:, at] = new
            top = jnp.maximum(top, jnp.abs(new))
        peaks[...] = top

    exponent = exponents(peaks[...])
    split = out_ref.shape[:2] + (GROUP,)
    out_ref[:, :, length:] = exponent.reshape(split).astype(jnp.int32).astype(jnp.int16)
    inverse = jnp.exp(exponent * (-LN2 / FINE)) * TOP

    @pl.loop(0, length // CHUNK)
    def _(i):
        for j in range(CHUNK // GROUP):
            at = lanes(i * CHUNK + j * GROUP)
            value = field[:, at].reshape(split)
            out_ref[:, :, at] = quantize(value, inverse.reshape(split))


def update(code, coeffs, reflector, half):
    parts, _, rows, width = code.shape
    length, reach = reflector.shape
    count = parts * rows
    return pl.pallas_call(
        update_kernel,
        grid=(1,),
        in_specs=[
            pl.BlockSpec((parts, None, rows, width), lambda i: (0, half, 0, 0)),
            pl.BlockSpec((parts, None, rows, 2 * reach), lambda i: (0, half, 0, 0)),
            pl.BlockSpec((length, reach), lambda i: (0, 0)),
        ],
        out_specs=pl.BlockSpec((parts, rows, width), lambda i: (0, 0, 0)),
        out_shape=jax.ShapeDtypeStruct((parts, rows, width), jnp.int16),
        scratch_shapes=[
            pltpu.VMEM((count, length), jnp.float32),
            pltpu.VMEM((count, GROUP), jnp.float32),
        ],
        compiler_params=pltpu.CompilerParams(vmem_limit_bytes=VMEM_LIMIT),
        cost_estimate=pl.CostEstimate(
            flops=4 * count * length * reach,
            bytes_accessed=4 * count * width + 2 * length * reach,
            transcendentals=0,
        ),
        name="update",
    )(code, coeffs, reflector)


def decode_kernel(code_ref, *refs):
    out_ref = refs[-1]
    length = out_ref.shape[1]
    steps = steps_of(code_ref[:, length:])

    @pl.loop(0, length // CHUNK)
    def _(i):
        for j, part in enumerate(decoded_chunk(code_ref, steps, i)):
            out_ref[:, lanes(i * CHUNK + j * GROUP)] = part


def decode(code, before, half):
    parts, rows, width = code.shape
    length = width - GROUP
    again = [] if before is None else [before]
    return pl.pallas_call(
        decode_kernel,
        grid=(parts,),
        in_specs=[pl.BlockSpec((None, rows, width), lambda i: (i, 0, 0))]
        + [pl.BlockSpec(memory_space=pl.ANY) for _ in again],
        out_specs=pl.BlockSpec((rows, length), lambda i: (half, i)),
        out_shape=jax.ShapeDtypeStruct((2 * rows, parts * length), jnp.float32),
        input_output_aliases={1: 0} if again else {},
        compiler_params=pltpu.CompilerParams(vmem_limit_bytes=VMEM_LIMIT),
        cost_estimate=pl.CostEstimate(
            flops=2 * parts * rows * length,
            bytes_accessed=6 * parts * rows * length,
            transcendentals=0,
        ),
        name="decode",
    )(code, *again)


def reflect_kernel(source_ref, shift_ref, *refs):
    pieces, reflector_ref, gram_ref = refs[:-2], refs[-2], refs[-1]
    rows, nb = pieces[0].shape
    first = pl.program_id(0) * rows
    gap = lax.broadcasted_iota(jnp.int32, (rows, nb), 0) - lax.broadcasted_iota(
        jnp.int32, (rows, nb), 1
    )
    for panel in range(PANELS):
        stored = pieces[0][...].astype(jnp.float32)
        for k in range(1, len(pieces)):
            other = pieces[k][...].astype(jnp.float32)
            stored = jnp.where(source_ref[panel] == k, other, stored)
        below = gap + (first - shift_ref[panel])
        unit = jnp.where(below == 0, 1.0, 0.0)
        block = jnp.where(below > 0, stored, unit).astype(jnp.bfloat16)
        reflector_ref[:, panel * nb : (panel + 1) * nb] = block
    block = reflector_ref[...]
    product = lax.dot_general(
        block, block, (((0,), (0,)), ((), ())), preferred_element_type=jnp.float32
    )

    @pl.when(pl.program_id(0) == 0)
    def _():
        gram_ref[...] = product

    @pl.when(pl.program_id(0) > 0)
    def _():
        gram_ref[...] += product


def reflect(pieces, source, shift):
    length, nb = pieces[0].shape
    rows, reach = min(CHUNK, length), PANELS * nb
    scalars = pl.BlockSpec(memory_space=pltpu.SMEM)
    return pl.pallas_call(
        reflect_kernel,
        grid=(length // rows,),
        in_specs=[scalars, scalars] + [pl.BlockSpec((rows, nb), lambda i: (i, 0)) for _ in pieces],
        out_specs=[
            pl.BlockSpec((rows, reach), lambda i: (i, 0)),
            pl.BlockSpec((reach, reach), lambda i: (0, 0)),
        ],
        out_shape=[
            jax.ShapeDtypeStruct((length, reach), jnp.bfloat16),
            jax.ShapeDtypeStruct((reach, reach), jnp.float32),
        ],
        compiler_params=pltpu.CompilerParams(vmem_limit_bytes=VMEM_LIMIT),
        cost_estimate=pl.CostEstimate(
            flops=2 * length * reach * reach, bytes_accessed=4 * length * reach, transcendentals=0
        ),
        name="reflect",
    )(source, shift, *pieces)


def solve_kernel(projection_ref, gram_ref, triangle_ref, out_ref):
    highest = lax.Precision.HIGHEST
    nb = triangle_ref.shape[1]
    reach = PANELS * nb
    coeffs = [None] * PANELS
    for panel in reversed(range(PANELS)):
        inner = projection_ref[:, panel * nb : (panel + 1) * nb]
        for later in range(panel + 1, PANELS):
            i, j = divmod(PAIRS.index((later, panel)), PANELS)
            block = gram_ref[i * nb : (i + 1) * nb, j * nb : (j + 1) * nb]
            inner = inner - jnp.dot(
                coeffs[later], block, precision=highest, preferred_element_type=jnp.float32
            )
        coeffs[panel] = lax.dot_general(
            inner,
            triangle_ref[panel].astype(jnp.float32),
            (((1,), (1,)), ((), ())),
            precision=highest,
            preferred_element_type=jnp.float32,
        )
        at = panel * nb
        high = coeffs[panel].astype(jnp.bfloat16)
        low = (coeffs[panel] - high.astype(jnp.float32)).astype(jnp.bfloat16)
        out_ref[:, at : at + nb] = high
        out_ref[:, reach + at : reach + at + nb] = low


def solve(projection, gram, triangles):
    count, reach = projection.shape
    return pl.pallas_call(
        solve_kernel,
        in_specs=[pl.BlockSpec(memory_space=pltpu.VMEM)] * 3,
        out_specs=pl.BlockSpec(memory_space=pltpu.VMEM),
        out_shape=jax.ShapeDtypeStruct((count, 2 * reach), jnp.bfloat16),
        compiler_params=pltpu.CompilerParams(vmem_limit_bytes=VMEM_LIMIT),
        name="solve",
    )(projection, gram, triangles)


def cut_panels(stored, n_col):
    length = stored.shape[0] // n_col
    me = lax.axis_index("col")
    return [
        lax.dynamic_slice_in_dim(stored, lax.rem(me + k, n_col) * length, length, axis=0)
        for k in range(n_col)
    ]


def spread_panels(pieces):
    n = len(pieces)
    return [
        lax.ppermute(piece, "col", [(i, (i + k) % n) for i in range(n)]) if k else piece
        for k, piece in enumerate(pieces)
    ]


def local(eigvecs, panels, tfactors, owners, offsets):
    both = ("row", "col")
    n_col = lax.axis_size("col")
    n_all = lax.axis_size("row") * n_col
    me = lax.axis_index("col")
    pieces, eigvecs = lax.optimization_barrier((cut_panels(panels[0], n_col), eigvecs))
    pieces = spread_panels(pieces)
    triangles = lax.all_gather(tfactors[0], "col")
    triangles = jnp.take(triangles, owners, axis=0)
    code = encode(eigvecs, n_all)
    code = lax.all_to_all(code, both, split_axis=0, concat_axis=0, tiled=True)
    code = code.reshape(-1, code.shape[-1])

    length, nb = pieces[0].shape
    first_row = (lax.axis_index("row") * n_col + me) * length
    reflector, gram = reflect(pieces, lax.rem(me - owners + n_col, n_col), offsets - first_row)
    blocks = [gram[q * nb : (q + 1) * nb, p * nb : (p + 1) * nb] for q, p in PAIRS]
    blocks += [jnp.zeros_like(blocks[0])] * (-len(blocks) % PANELS)
    packed = [
        jnp.concatenate(blocks[i : i + PANELS], axis=1) for i in range(0, len(blocks), PANELS)
    ]
    packed = jnp.concatenate(packed, axis=0)

    count = code.shape[0]
    rows = min(count, 256)
    projection = project(code, reflector, rows)
    own = count // n_all
    sums = jnp.concatenate(
        [projection.reshape(n_all, own, -1), packed.reshape(n_all, -1, packed.shape[1])], axis=1
    )
    sums = lax.all_to_all(sums, both, split_axis=0, concat_axis=0, tiled=True)
    sums = jnp.sum(sums, axis=0)
    sums = jnp.broadcast_to(sums[None], (n_all,) + sums.shape)
    sums = lax.all_to_all(sums, both, split_axis=0, concat_axis=0, tiled=True)
    coeffs = solve(
        sums[:, :own].reshape(projection.shape), sums[:, own:].reshape(packed.shape), triangles
    )
    split = (n_col, 2, count // (2 * n_col), -1)
    code, coeffs = code.reshape(split), coeffs.reshape(split)
    back = None
    for half in range(2):
        part = update(code, coeffs, reflector, half)
        part = lax.all_to_all(part, "col", split_axis=0, concat_axis=0, tiled=True)
        back = decode(part, back, half)
    return back


def solution(mesh):
    in_specs = (P(("row", "col"), None), P("col", "row", None), P("col", None, None), P(), P())
    out_specs = P("col", "row")
    return jax.shard_map(local, mesh=mesh, in_specs=in_specs, out_specs=out_specs, check_vma=False)
```

```python
import jax
import jax.numpy as jnp
from jax import lax
from jax.experimental import pallas as pl
from jax.experimental.pallas import tpu as pltpu
from jax.sharding import PartitionSpec as P

PANELS = 4
GROUP = 128
CHUNK = 1024
TOP = 32760.0
FINE = 256.0
LN2 = 0.6931471805599453
PAIRS = [(q, p) for p in range(PANELS) for q in range(p + 1, PANELS)]
VMEM_LIMIT = 56 * 1024 * 1024


def exponents(peaks):
    return jnp.ceil(jnp.log(jnp.maximum(peaks, 1e-30)) * (FINE / LN2))


def steps_of(code):
    return jnp.exp(code.astype(jnp.int32).astype(jnp.float32) * (LN2 / FINE)) * (1.0 / TOP)


def quantize(value, inverse):
    return ((value * inverse + 32768.5).astype(jnp.int32) - 32768).astype(jnp.int16)


def as_float(code):
    return code.astype(jnp.int32).astype(jnp.float32)


def encode_kernel(x_ref, code_ref):
    parts, rows, width = code_ref.shape
    length = width - GROUP

    @pl.loop(0, parts)
    def _(part):
        peaks = jnp.zeros((rows, GROUP), jnp.float32)
        for g in range(length // GROUP):
            peaks = jnp.maximum(peaks, jnp.abs(x_ref[:, lanes(part * length + g * GROUP)]))
        exponent = exponents(peaks)
        code_ref[part, :, length:] = exponent.astype(jnp.int32).astype(jnp.int16)
        inverse = jnp.exp(exponent * (-LN2 / FINE)) * TOP
        for g in range(length // GROUP):
            value = x_ref[:, lanes(part * length + g * GROUP)]
            code_ref[part, :, g * GROUP : (g + 1) * GROUP] = quantize(value, inverse)


def encode(eigvecs, parts):
    rows, columns = eigvecs.shape
    length = columns // parts
    at_once = 4 if parts % 4 == 0 else 1
    return pl.pallas_call(
        encode_kernel,
        grid=(parts // at_once,),
        in_specs=[pl.BlockSpec((rows, at_once * length), lambda i: (0, i))],
        out_specs=pl.BlockSpec((at_once, rows, length + GROUP), lambda i: (i, 0, 0)),
        out_shape=jax.ShapeDtypeStruct((parts, rows, length + GROUP), jnp.int16),
        compiler_params=pltpu.CompilerParams(vmem_limit_bytes=VMEM_LIMIT),
        cost_estimate=pl.CostEstimate(
            flops=6 * rows * columns, bytes_accessed=6 * rows * columns, transcendentals=0
        ),
        name="encode",
    )(eigvecs)


def lanes(start):
    return pl.ds(pl.multiple_of(start, GROUP), GROUP)


def decoded_chunk(code_ref, steps, i):
    return [
        as_float(code_ref[:, lanes(i * CHUNK + j * GROUP)]) * steps
        for j in range(CHUNK // GROUP)
    ]


def project_kernel(code_ref, reflector_ref, out_ref, total):
    rows, length = out_ref.shape[0], reflector_ref.shape[0]
    steps = steps_of(code_ref[:, length:])
    total[...] = jnp.zeros_like(total)

    @pl.loop(0, length // CHUNK, unroll=2)
    def _(i):
        value = jnp.concatenate(decoded_chunk(code_ref, steps, i), axis=1)
        high = value.astype(jnp.bfloat16)
        low = (value - high.astype(jnp.float32)).astype(jnp.bfloat16)
        block = reflector_ref[pl.ds(pl.multiple_of(i * CHUNK, CHUNK), CHUNK), :]
        total[...] += jnp.dot(
            jnp.concatenate([high, low], axis=0), block, preferred_element_type=jnp.float32
        )

    out_ref[...] = total[:rows] + total[rows:]


def project(code, reflector, rows):
    count, width = code.shape
    length, reach = reflector.shape
    return pl.pallas_call(
        project_kernel,
        grid=(count // rows,),
        in_specs=[
            pl.BlockSpec((rows, width), lambda i: (i, 0)),
            pl.BlockSpec((length, reach), lambda i: (0, 0)),
        ],
        out_specs=pl.BlockSpec((rows, reach), lambda i: (i, 0)),
        out_shape=jax.ShapeDtypeStruct((count, reach), jnp.float32),
        scratch_shapes=[pltpu.VMEM((2 * rows, reach), jnp.float32)],
        compiler_params=pltpu.CompilerParams(vmem_limit_bytes=VMEM_LIMIT),
        cost_estimate=pl.CostEstimate(
            flops=4 * count * length * reach,
            bytes_accessed=2 * count * width + 2 * length * reach,
            transcendentals=0,
        ),
        name="project",
    )(code, reflector)


def update_kernel(code_ref, coeff_ref, reflector_ref, out_ref, field, peaks):
    rows, length = field.shape
    reach = reflector_ref.shape[1]

    def joined(value):
        return value.reshape(rows, value.shape[-1])

    steps = joined(steps_of(code_ref[:, :, length:]))
    coeffs = jnp.concatenate(
        [joined(coeff_ref[:, :, :reach]), joined(coeff_ref[:, :, reach:])], axis=0
    )
    peaks[...] = jnp.zeros_like(peaks)

    @pl.loop(0, length // CHUNK, unroll=2)
    def _(i):
        block = reflector_ref[pl.ds(pl.multiple_of(i * CHUNK, CHUNK), CHUNK), :]
        change = lax.dot_general(
            coeffs, block, (((1,), (1,)), ((), ())), preferred_element_type=jnp.float32
        )
        change = change[:rows] + change[rows:]
        top = peaks[...]
        for j in range(CHUNK // GROUP):
            at = lanes(i * CHUNK + j * GROUP)
            part = joined(as_float(code_ref[:, :, at])) * steps
            new = part - change[:, j * GROUP : (j + 1) * GROUP]
            field[:, at] = new
            top = jnp.maximum(top, jnp.abs(new))
        peaks[...] = top

    exponent = exponents(peaks[...])
    split = out_ref.shape[:2] + (GROUP,)
    out_ref[:, :, length:] = exponent.reshape(split).astype(jnp.int32).astype(jnp.int16)
    inverse = jnp.exp(exponent * (-LN2 / FINE)) * TOP

    @pl.loop(0, length // CHUNK, unroll=2)
    def _(i):
        for j in range(CHUNK // GROUP):
            at = lanes(i * CHUNK + j * GROUP)
            value = field[:, at].reshape(split)
            out_ref[:, :, at] = quantize(value, inverse.reshape(split))


def update(code, coeffs, reflector, half):
    parts, _, rows, width = code.shape
    length, reach = reflector.shape
    count = parts * rows
    return pl.pallas_call(
        update_kernel,
        grid=(1,),
        in_specs=[
            pl.BlockSpec((parts, None, rows, width), lambda i: (0, half, 0, 0)),
            pl.BlockSpec((parts, None, rows, 2 * reach), lambda i: (0, half, 0, 0)),
            pl.BlockSpec((length, reach), lambda i: (0, 0)),
        ],
        out_specs=pl.BlockSpec((parts, rows, width), lambda i: (0, 0, 0)),
        out_shape=jax.ShapeDtypeStruct((parts, rows, width), jnp.int16),
        scratch_shapes=[
            pltpu.VMEM((count, length), jnp.float32),
            pltpu.VMEM((count, GROUP), jnp.float32),
        ],
        compiler_params=pltpu.CompilerParams(vmem_limit_bytes=VMEM_LIMIT),
        cost_estimate=pl.CostEstimate(
            flops=4 * count * length * reach,
            bytes_accessed=4 * count * width + 2 * length * reach,
            transcendentals=0,
        ),
        name="update",
    )(code, coeffs, reflector)


def decode_kernel(code_ref, *refs):
    out_ref = refs[-1]
    length = out_ref.shape[1]
    steps = steps_of(code_ref[:, length:])

    @pl.loop(0, length // CHUNK)
    def _(i):
        for j, part in enumerate(decoded_chunk(code_ref, steps, i)):
            out_ref[:, lanes(i * CHUNK + j * GROUP)] = part


def decode(code, before, half):
    parts, rows, width = code.shape
    length = width - GROUP
    again = [] if before is None else [before]
    return pl.pallas_call(
        decode_kernel,
        grid=(parts,),
        in_specs=[pl.BlockSpec((None, rows, width), lambda i: (i, 0, 0))]
        + [pl.BlockSpec(memory_space=pl.ANY) for _ in again],
        out_specs=pl.BlockSpec((rows, length), lambda i: (half, i)),
        out_shape=jax.ShapeDtypeStruct((2 * rows, parts * length), jnp.float32),
        input_output_aliases={1: 0} if again else {},
        compiler_params=pltpu.CompilerParams(vmem_limit_bytes=VMEM_LIMIT),
        cost_estimate=pl.CostEstimate(
            flops=2 * parts * rows * length,
            bytes_accessed=6 * parts * rows * length,
            transcendentals=0,
        ),
        name="decode",
    )(code, *again)


def reflect_kernel(source_ref, shift_ref, *refs):
    pieces, reflector_ref, gram_ref = refs[:-2], refs[-2], refs[-1]
    rows, nb = pieces[0].shape
    first = pl.program_id(0) * rows
    gap = lax.broadcasted_iota(jnp.int32, (rows, nb), 0) - lax.broadcasted_iota(
        jnp.int32, (rows, nb), 1
    )
    for panel in range(PANELS):
        stored = pieces[0][...].astype(jnp.float32)
        for k in range(1, len(pieces)):
            other = pieces[k][...].astype(jnp.float32)
            stored = jnp.where(source_ref[panel] == k, other, stored)
        below = gap + (first - shift_ref[panel])
        unit = jnp.where(below == 0, 1.0, 0.0)
        block = jnp.where(below > 0, stored, unit).astype(jnp.bfloat16)
        reflector_ref[:, panel * nb : (panel + 1) * nb] = block
    product = lax.dot_general(
        reflector_ref[:, nb:],
        reflector_ref[:, :-nb],
        (((0,), (0,)), ((), ())),
        preferred_element_type=jnp.float32,
    )

    @pl.when(pl.program_id(0) == 0)
    def _():
        gram_ref[...] = product

    @pl.when(pl.program_id(0) > 0)
    def _():
        gram_ref[...] += product


def reflect(pieces, source, shift):
    length, nb = pieces[0].shape
    rows, reach = min(CHUNK, length), PANELS * nb
    scalars = pl.BlockSpec(memory_space=pltpu.SMEM)
    return pl.pallas_call(
        reflect_kernel,
        grid=(length // rows,),
        in_specs=[scalars, scalars] + [pl.BlockSpec((rows, nb), lambda i: (i, 0)) for _ in pieces],
        out_specs=[
            pl.BlockSpec((rows, reach), lambda i: (i, 0)),
            pl.BlockSpec((reach - nb, reach - nb), lambda i: (0, 0)),
        ],
        out_shape=[
            jax.ShapeDtypeStruct((length, reach), jnp.bfloat16),
            jax.ShapeDtypeStruct((reach - nb, reach - nb), jnp.float32),
        ],
        compiler_params=pltpu.CompilerParams(vmem_limit_bytes=VMEM_LIMIT),
        cost_estimate=pl.CostEstimate(
            flops=2 * length * reach * reach, bytes_accessed=4 * length * reach, transcendentals=0
        ),
        name="reflect",
    )(source, shift, *pieces)


def solve_kernel(projection_ref, gram_ref, triangle_ref, out_ref):
    highest = lax.Precision.HIGHEST
    nb = triangle_ref.shape[1]
    reach = PANELS * nb
    coeffs = [None] * PANELS
    for panel in reversed(range(PANELS)):
        inner = projection_ref[:, panel * nb : (panel + 1) * nb]
        for later in range(panel + 1, PANELS):
            i, j = divmod(PAIRS.index((later, panel)), PANELS)
            block = gram_ref[i * nb : (i + 1) * nb, j * nb : (j + 1) * nb]
            inner = inner - jnp.dot(
                coeffs[later], block, precision=highest, preferred_element_type=jnp.float32
            )
        coeffs[panel] = lax.dot_general(
            inner,
            triangle_ref[panel].astype(jnp.float32),
            (((1,), (1,)), ((), ())),
            precision=highest,
            preferred_element_type=jnp.float32,
        )
        at = panel * nb
        high = coeffs[panel].astype(jnp.bfloat16)
        low = (coeffs[panel] - high.astype(jnp.float32)).astype(jnp.bfloat16)
        out_ref[:, at : at + nb] = high
        out_ref[:, reach + at : reach + at + nb] = low


def solve(projection, gram, triangles):
    count, reach = projection.shape
    return pl.pallas_call(
        solve_kernel,
        in_specs=[pl.BlockSpec(memory_space=pltpu.VMEM)] * 3,
        out_specs=pl.BlockSpec(memory_space=pltpu.VMEM),
        out_shape=jax.ShapeDtypeStruct((count, 2 * reach), jnp.bfloat16),
        compiler_params=pltpu.CompilerParams(vmem_limit_bytes=VMEM_LIMIT),
        name="solve",
    )(projection, gram, triangles)


def cut_panels(stored, n_col):
    length = stored.shape[0] // n_col
    me = lax.axis_index("col")
    return [
        lax.dynamic_slice_in_dim(stored, lax.rem(me + k, n_col) * length, length, axis=0)
        for k in range(n_col)
    ]


def spread_panels(pieces):
    n = len(pieces)
    return [
        lax.ppermute(piece, "col", [(i, (i + k) % n) for i in range(n)]) if k else piece
        for k, piece in enumerate(pieces)
    ]


def local(eigvecs, panels, tfactors, owners, offsets):
    both = ("row", "col")
    n_col = lax.axis_size("col")
    n_all = lax.axis_size("row") * n_col
    me = lax.axis_index("col")
    pieces = spread_panels(cut_panels(panels[0], n_col))
    triangles = lax.all_gather(tfactors[0], "col")
    triangles = jnp.take(triangles, owners, axis=0)
    code = encode(eigvecs, n_all)
    code = lax.all_to_all(code, both, split_axis=0, concat_axis=0, tiled=True)
    code = code.reshape(-1, code.shape[-1])

    length, nb = pieces[0].shape
    first_row = (lax.axis_index("row") * n_col + me) * length
    reflector, gram = reflect(pieces, lax.rem(me - owners + n_col, n_col), offsets - first_row)
    blocks = [gram[(q - 1) * nb : q * nb, p * nb : (p + 1) * nb] for q, p in PAIRS]
    blocks += [jnp.zeros_like(blocks[0])] * (-len(blocks) % PANELS)
    packed = [
        jnp.concatenate(blocks[i : i + PANELS], axis=1) for i in range(0, len(blocks), PANELS)
    ]
    packed = jnp.concatenate(packed, axis=0)

    count = code.shape[0]
    rows = min(count, 256)
    projection = project(code, reflector, rows)
    own = count // n_all
    sums = jnp.concatenate(
        [projection.reshape(n_all, own, -1), packed.reshape(n_all, -1, packed.shape[1])], axis=1
    )
    sums = lax.all_to_all(sums, both, split_axis=0, concat_axis=0, tiled=True)
    sums = jnp.sum(sums, axis=0)
    sums = jnp.broadcast_to(sums[None], (n_all,) + sums.shape)
    sums = lax.all_to_all(sums, both, split_axis=0, concat_axis=0, tiled=True)
    coeffs = solve(
        sums[:, :own].reshape(projection.shape), sums[:, own:].reshape(packed.shape), triangles
    )
    split = (n_col, 2, count // (2 * n_col), -1)
    code, coeffs = code.reshape(split), coeffs.reshape(split)
    back = None
    for half in range(2):
        part = update(code, coeffs, reflector, half)
        part = lax.all_to_all(part, "col", split_axis=0, concat_axis=0, tiled=True)
        back = decode(part, back, half)
    return back


def solution(mesh):
    in_specs = (P(("row", "col"), None), P("col", "row", None), P("col", None, None), P(), P())
    out_specs = P("col", "row")
    return jax.shard_map(local, mesh=mesh, in_specs=in_specs, out_specs=out_specs, check_vma=False)
```
